32 devices in a mesh: pipe: 4 (over z), expert: 8 (over y, x, core).
Axes of the slice: x: 2, y: 2, z: 4, core: 2. Of those that a mesh axis runs over, the one named last changes fastest.
Arguments:
- tokens: bfloat16 [4096, 3584], P(('pipe', 'expert')), may hold values from -6 to 6
- out_grad: bfloat16 [4096, 3584], P(('pipe', 'expert')), may hold values from -6 to 6
- probs: bfloat16 [4096, 8], P(('pipe', 'expert')), may hold values from 0.049804688 to 1
- expert_ids: int32 [4096, 8], P(('pipe', 'expert')), may hold values from 0 to 255, as said below
- w_gate: bfloat16 [4, 3584, 2048], P('pipe', None, 'expert'), as said below
- w_up: bfloat16 [4, 3584, 2048], P('pipe', None, 'expert'), as said below
- w_down: bfloat16 [4, 2048, 3584], P('pipe', 'expert'), as said below
Outputs:
- tokens_grad: bfloat16 [4096, 3584], P(('pipe', 'expert'))
- weight_grads: bfloat16 [4, 3, 1792, 2048], P('pipe', None, None, 'expert')
The draws below stay inside these ranges and needn't reach their ends.
Inputs may be any that keep to these rules, and one draw needn't show every extreme that they name: `expert_ids`: each row names 8 different experts. Experts 1 and above lie outside this window. Among the 128 tokens of one device (aligned blocks of rows), each expert below 1 is named by at most 8 tokens, and in every draw one such expert is named by exactly 8 tokens on every device. `w_gate`: entries k and 3 - k along the first dimension are equal. `w_up`: entries k and 3 - k along the first dimension are equal. `w_down`: entries k and 3 - k along the first dimension are equal.
All inputs are finite; a program needn't handle non-finite values.
Results may differ from the reference program's by a relative error of at most 0.0065.
Values may be sent and summed in bfloat16 or wider, within the bound.
A program may use at most 128 MiB of HBM per device.

```python
import math
import jax
import jax.numpy as jnp
from jax import lax

D = 3584
H = 2048
EXPERTS = 256
TOP = 8
TOK_DEV = 128
CAP = 8
EXP_FLIGHT = 1
TOKENS = 4096
N_PIPE = 4
N_EXPERT = 8


def draw_expert_ids(key, part):
    blocks = TOKENS // TOK_DEV
    key_hot, key_count, key_order, key_offset, key_turn = jax.random.split(key, 5)
    hottest = jax.random.randint(key_hot, (), 0, EXP_FLIGHT)
    counts = jax.random.randint(key_count, (blocks, EXP_FLIGHT), 0, CAP + 1)
    counts = jnp.where(jnp.arange(EXP_FLIGHT)[None, :] == hottest, CAP, counts)
    order_keys = jax.random.split(key_order, blocks * EXP_FLIGHT)
    orders = jax.vmap(lambda single: jax.random.permutation(single, TOK_DEV))(order_keys)
    orders = orders.reshape(blocks, EXP_FLIGHT, TOK_DEV)
    chosen = orders < counts[:, :, None]
    chosen = jnp.transpose(chosen, (0, 2, 1)).reshape(TOKENS, EXP_FLIGHT)
    chosen = jnp.pad(chosen, ((0, 0), (0, TOP - EXP_FLIGHT)))
    outside = EXPERTS - EXP_FLIGHT
    offset = jax.random.randint(key_offset, (TOKENS, 1), 0, outside)
    column = jnp.arange(TOP)[None, :]
    listed = jnp.where(chosen, column, EXP_FLIGHT + (offset + column) % outside)
    turn = jax.random.randint(key_turn, (TOKENS, 1), 0, TOP)
    gather_index = (column - turn) % TOP
    return jnp.take_along_axis(listed, gather_index, axis=1).astype(jnp.int32)


def mirrored_weight(key, rows, columns, fan_in):
    sections = N_PIPE // 2
    base = jax.random.normal(key, (sections, rows, columns), jnp.float32) * float(fan_in) ** (-0.5)
    ranks = jnp.arange(N_PIPE)
    section_of = jnp.minimum(ranks, N_PIPE - 1 - ranks)
    return base[section_of]


def draw_w_gate(key, part):
    return mirrored_weight(jax.random.fold_in(key, 11), D, EXP_FLIGHT * H, D).astype(jnp.bfloat16)


def draw_w_up(key, part):
    return mirrored_weight(jax.random.fold_in(key, 23), D, EXP_FLIGHT * H, D).astype(jnp.bfloat16)


def draw_w_down(key, part):
    return mirrored_weight(jax.random.fold_in(key, 37), EXP_FLIGHT * H, D, H).astype(jnp.bfloat16)


def shard_levels(rng, shape, shards, least, high):
    loudness = 1.0
    for dim, parts in shards:
        heights = jax.random.uniform(jax.random.fold_in(jax.random.fold_in(rng, 6), dim), (parts,), jnp.float32, least / len(shards), high / len(shards))
        loudness = loudness * jnp.repeat(jnp.exp(heights), shape[dim] // parts).reshape((-1,) + (1,) * (len(shape) - 1 - dim))
    return loudness


def centred(rng, shape, deviation, bound, cuts=(), kind=jnp.bfloat16):
    values = deviation * jax.random.normal(rng, shape, jnp.float32)
    if cuts:
        values = values * shard_levels(rng, shape, cuts, -0.22, 0.18)
    return jnp.clip(values, -bound, bound).astype(kind)


def setup_inputs(seed: int = 0) -> dict:
    splits = jax.random.split(jax.random.key(seed), 8)
    tokens = centred(splits[0], (TOKENS, D), 1.0, 6.0, ((0, 32),))
    out_grad = centred(splits[1], (TOKENS, D), 1.0, 6.0, ((0, 32),))
    probs = jnp.clip(jnp.exp(math.log(1.0) - 2.9996462 * jax.random.uniform(splits[2], (TOKENS, TOP), jnp.float32) ** shard_levels(splits[2], (TOKENS, TOP), ((0, 32),), -0.2, 0.2)), 0.049804688, 1.0).astype(jnp.bfloat16)
    expert_ids = draw_expert_ids(jax.random.fold_in(splits[7], 71), 0)
    w_gate = draw_w_gate(jax.random.fold_in(splits[7], 71), 0)
    w_up = draw_w_up(jax.random.fold_in(splits[7], 71), 0)
    w_down = draw_w_down(jax.random.fold_in(splits[7], 71), 0)
    return dict(tokens=tokens, out_grad=out_grad, probs=probs, expert_ids=expert_ids, w_gate=w_gate, w_up=w_up, w_down=w_down)


def route_slots(block_ids, block_probs, in_flight):
    experts = jnp.arange(in_flight, dtype=jnp.int32)
    hits = block_ids[:, :, None] == experts[None, None, :]
    member = jnp.any(hits, axis=1).astype(jnp.int32)
    chosen = jnp.sum(jnp.where(hits, block_probs.astype(jnp.float32)[:, :, None], jnp.float32(0.0)), axis=1)
    position = (jnp.cumsum(member, axis=0) - member).astype(jnp.int32)
    slots = jnp.arange(CAP, dtype=jnp.int32)
    select = (member.T[:, None, :] == 1) & (position.T[:, None, :] == slots[None, :, None])
    select = select.astype(jnp.float32)
    slot_weight = jnp.einsum("ect,te->ec", select, chosen, precision=lax.Precision.HIGHEST)
    return select.reshape(in_flight * CAP, -1), slot_weight.reshape(in_flight * CAP)


def expert_backward(operands):
    x_rows, grad_rows, gate_cols, up_cols, down_rows = operands
    gate = jnp.dot(x_rows, gate_cols, preferred_element_type=jnp.float32)
    up = jnp.dot(x_rows, up_cols, preferred_element_type=jnp.float32)
    sigmoid_gate = jax.nn.sigmoid(gate)
    activated = gate * sigmoid_gate
    hidden = (activated * up).astype(jnp.bfloat16)
    back = jnp.dot(grad_rows, down_rows.T, preferred_element_type=jnp.float32)
    d_gate = (back * up * sigmoid_gate * (1.0 + gate * (1.0 - sigmoid_gate))).astype(jnp.bfloat16)
    d_up = (back * activated).astype(jnp.bfloat16)
    row_grad = jnp.dot(d_gate, gate_cols.T, preferred_element_type=jnp.float32) + jnp.dot(d_up, up_cols.T, preferred_element_type=jnp.float32)
    grads = jnp.stack([
        jnp.dot(x_rows.T, d_gate, preferred_element_type=jnp.float32),
        jnp.dot(x_rows.T, d_up, preferred_element_type=jnp.float32),
        jnp.dot(grad_rows.T, hidden, preferred_element_type=jnp.float32),
    ]).astype(jnp.bfloat16)
    return row_grad, grads


def reference(tokens, out_grad, probs, expert_ids, w_gate, w_up, w_down):
    in_flight = EXP_FLIGHT
    blocks = N_PIPE * N_EXPERT

    def prepare(block_tokens, block_grad, block_probs, block_ids):
        select, slot_weight = route_slots(block_ids, block_probs, in_flight)
        picker = select.astype(jnp.bfloat16)
        x_rows = jnp.dot(picker, block_tokens, preferred_element_type=jnp.float32).astype(jnp.bfloat16)
        grad_rows = (jnp.dot(picker, block_grad, preferred_element_type=jnp.float32) * slot_weight[:, None]).astype(jnp.bfloat16)
        return select, x_rows, grad_rows

    select, x_rows, grad_rows = jax.vmap(prepare)(
        tokens.reshape(blocks, TOK_DEV, D), out_grad.reshape(blocks, TOK_DEV, D),
        probs.reshape(blocks, TOK_DEV, TOP), expert_ids.reshape(blocks, TOK_DEV, TOP))

    def by_expert(rows):
        rows = rows.reshape(N_PIPE, N_EXPERT, in_flight, CAP, D).transpose(0, 2, 1, 3, 4)
        return rows.reshape(N_PIPE * in_flight, N_EXPERT * CAP, D)

    gate_cols = w_gate.reshape(N_PIPE, D, in_flight, H).transpose(0, 2, 1, 3).reshape(N_PIPE * in_flight, D, H)
    up_cols = w_up.reshape(N_PIPE, D, in_flight, H).transpose(0, 2, 1, 3).reshape(N_PIPE * in_flight, D, H)
    down_rows = w_down.reshape(N_PIPE * in_flight, H, D)
    row_grad, grads = lax.map(expert_backward, (by_expert(x_rows), by_expert(grad_rows), gate_cols, up_cols, down_rows))

    row_grad = row_grad.reshape(N_PIPE, in_flight, N_EXPERT, CAP, D).transpose(0, 2, 1, 3, 4).reshape(blocks, in_flight * CAP, D)
    tokens_grad = jnp.einsum("bst,bsd->btd", select, row_grad, precision=lax.Precision.HIGHEST)
    tokens_grad = tokens_grad.astype(jnp.bfloat16).reshape(TOKENS, D)

    grads = grads.reshape(N_PIPE, in_flight, 3, D, H).transpose(0, 2, 3, 1, 4).reshape(N_PIPE, 3, D, in_flight * H)
    mirrored = grads[::-1]
    half_rows = D // 2
    half_pipe = N_PIPE // 2
    lower = (grads[:half_pipe, :, :half_rows].astype(jnp.float32) + mirrored[:half_pipe, :, :half_rows].astype(jnp.float32)).astype(jnp.bfloat16)
    upper = (grads[half_pipe:, :, half_rows:].astype(jnp.float32) + mirrored[half_pipe:, :, half_rows:].astype(jnp.float32)).astype(jnp.bfloat16)
    weight_grads = jnp.concatenate([lower, upper], axis=0)
    return tokens_grad, weight_grads
```

```python
import jax
import jax.numpy as jnp
from jax import lax
from jax.sharding import PartitionSpec as P

GROUP = 8
CAP = 8


def route_slots(block_ids, block_probs, in_flight):
    experts = jnp.arange(in_flight, dtype=jnp.int32)
    hits = block_ids[:, :, None] == experts[None, None, :]
    member = jnp.any(hits, axis=1).astype(jnp.int32)
    chosen = jnp.sum(
        jnp.where(hits, block_probs.astype(jnp.float32)[:, :, None], jnp.float32(0.0)), axis=1
    )
    position = jnp.cumsum(member, axis=0) - member
    slots = jnp.arange(CAP, dtype=jnp.int32)
    select = (member.T[:, None, :] == 1) & (position.T[:, None, :] == slots[None, :, None])
    select = select.astype(jnp.float32)
    slot_weight = jnp.einsum("ect,te->ec", select, chosen, precision=lax.Precision.HIGHEST)
    return (select.reshape(in_flight * CAP, -1), slot_weight.reshape(in_flight * CAP))


def contract(left, right, left_dim, right_dim):
    return lax.dot_general(
        left, right, (((left_dim,), (right_dim,)), ((), ())), preferred_element_type=jnp.float32
    )


def to_mirror(value):
    count = lax.axis_size("pipe")
    return lax.ppermute(value, "pipe", [(k, count - 1 - k) for k in range(count)])


def expert_activations(x_rows, grad_rows, gate_cols, up_cols, down_rows):
    gate = jnp.dot(x_rows, gate_cols, preferred_element_type=jnp.float32)
    up = jnp.dot(x_rows, up_cols, preferred_element_type=jnp.float32)
    sigmoid_gate = jax.nn.sigmoid(gate)
    activated = gate * sigmoid_gate
    hidden = (activated * up).astype(jnp.bfloat16)
    back = contract(grad_rows, down_rows, 1, 1)
    d_gate = (back * up * sigmoid_gate * (1.0 + gate * (1.0 - sigmoid_gate))).astype(jnp.bfloat16)
    d_up = (back * activated).astype(jnp.bfloat16)
    return d_gate, d_up, hidden


def body(tokens, out_grad, probs, expert_ids, w_gate, w_up, w_down):
    axis_width = lax.axis_size("expert")
    in_flight = axis_width // GROUP
    features = tokens.shape[1]
    half = features // 2
    lower = lax.axis_index("pipe") < lax.axis_size("pipe") // 2
    select, slot_weight = route_slots(expert_ids, probs, in_flight)
    picker = select.astype(jnp.bfloat16)
    x_rows = jnp.dot(picker, tokens, preferred_element_type=jnp.float32).astype(jnp.bfloat16)
    grad_rows = (
        jnp.dot(picker, out_grad, preferred_element_type=jnp.float32) * slot_weight[:, None]
    ).astype(jnp.bfloat16)
    stacked = jnp.stack([x_rows, grad_rows])
    mirrored = to_mirror(jnp.where(lower, stacked[:, :, half:], stacked[:, :, :half]))

    def spread(rows):
        width = rows.shape[-1]
        rows = jnp.broadcast_to(
            rows.reshape(2, in_flight, 1, CAP, width), (2, in_flight, GROUP, CAP, width)
        ).reshape(2, axis_width, CAP, width)
        rows = lax.all_to_all(rows, "expert", split_axis=1, concat_axis=1, tiled=True)
        return rows.reshape(2, axis_width * CAP, width)

    arrived = spread(stacked)
    d_gate, d_up, hidden = expert_activations(
        arrived[0], arrived[1], w_gate[0], w_up[0], w_down[0]
    )
    activations = jnp.stack([d_gate, d_up, hidden])
    other_activations = to_mirror(activations)
    row_grad = contract(d_gate, w_gate[0], 1, 1) + contract(d_up, w_up[0], 1, 1)
    returned = lax.all_to_all(
        row_grad.reshape(axis_width, CAP, features),
        "expert",
        split_axis=0,
        concat_axis=0,
        tiled=True,
    )
    summed = jnp.sum(returned.reshape(in_flight, GROUP, CAP, features), axis=1).reshape(
        in_flight * CAP, features
    )
    tokens_grad = lax.dot_general(
        select,
        summed,
        (((0,), (0,)), ((), ())),
        precision=lax.Precision.HIGHEST,
        preferred_element_type=jnp.float32,
    )
    tokens_grad = tokens_grad.astype(jnp.bfloat16)
    other = spread(mirrored)
    kept = jnp.where(lower, arrived[:, :, :half], arrived[:, :, half:])
    rows = jnp.concatenate([kept, other], axis=1)
    right = jnp.concatenate([activations, other_activations], axis=1)
    weight_grads = jnp.stack(
        [
            contract(rows[0], right[0], 0, 0),
            contract(rows[0], right[1], 0, 0),
            contract(rows[1], right[2], 0, 0),
        ]
    ).astype(jnp.bfloat16)
    return (tokens_grad, weight_grads[None])


def solution(mesh):
    return jax.shard_map(
        body,
        mesh=mesh,
        in_specs=(
            P(("pipe", "expert"), None),
            P(("pipe", "expert"), None),
            P(("pipe", "expert"), None),
            P(("pipe", "expert"), None),
            P("pipe", None, "expert"),
            P("pipe", None, "expert"),
            P("pipe", "expert", None),
        ),
        out_specs=(P(("pipe", "expert"), None), P("pipe", None, None, "expert")),
        check_vma=False,
    )
```

```python
import jax
import jax.numpy as jnp
from jax import lax
from jax.experimental import pallas as pl
from jax.experimental.pallas import tpu as pltpu
from jax.sharding import PartitionSpec as P

GROUP = 8
CAP = 8
MESH = pl.DeviceIdType.MESH
TILE = 256


def route_slots(block_ids, block_probs, in_flight):
    experts = jnp.arange(in_flight, dtype=jnp.int32)
    hits = block_ids[:, :, None] == experts[None, None, :]
    member = jnp.any(hits, axis=1).astype(jnp.int32)
    chosen = jnp.sum(
        jnp.where(hits, block_probs.astype(jnp.float32)[:, :, None], jnp.float32(0.0)), axis=1
    )
    position = jnp.cumsum(member, axis=0) - member
    slots = jnp.arange(CAP, dtype=jnp.int32)
    select = (member.T[:, None, :] == 1) & (position.T[:, None, :] == slots[None, :, None])
    select = select.astype(jnp.float32)
    slot_weight = jnp.einsum("ect,te->ec", select, chosen, precision=lax.Precision.HIGHEST)
    return (select.reshape(in_flight * CAP, -1), slot_weight.reshape(in_flight * CAP))


def contract(left, right, left_dim, right_dim):
    return lax.dot_general(
        left, right, (((left_dim,), (right_dim,)), ((), ())), preferred_element_type=jnp.float32
    )


def to_mirror(value):
    count = lax.axis_size("pipe")
    return lax.ppermute(value, "pipe", [(k, count - 1 - k) for k in range(count)])


def expert_activations(x_rows, grad_rows, gate_cols, up_cols, down_rows):
    gate = jnp.dot(x_rows, gate_cols, preferred_element_type=jnp.float32)
    up = jnp.dot(x_rows, up_cols, preferred_element_type=jnp.float32)
    sigmoid_gate = jax.nn.sigmoid(gate)
    activated = gate * sigmoid_gate
    hidden = (activated * up).astype(jnp.bfloat16)
    back = contract(grad_rows, down_rows, 1, 1)
    d_gate = (back * up * sigmoid_gate * (1.0 + gate * (1.0 - sigmoid_gate))).astype(jnp.bfloat16)
    d_up = (back * activated).astype(jnp.bfloat16)
    return d_gate, d_up, hidden


def body(tokens, out_grad, probs, expert_ids, w_gate, w_up, w_down):
    axis_width = lax.axis_size("expert")
    in_flight = axis_width // GROUP
    features = tokens.shape[1]
    half = features // 2
    lower = lax.axis_index("pipe") < lax.axis_size("pipe") // 2
    select, slot_weight = route_slots(expert_ids, probs, in_flight)
    picker = select.astype(jnp.bfloat16)
    x_rows = jnp.dot(picker, tokens, preferred_element_type=jnp.float32).astype(jnp.bfloat16)
    grad_rows = (
        jnp.dot(picker, out_grad, preferred_element_type=jnp.float32) * slot_weight[:, None]
    ).astype(jnp.bfloat16)
    stacked = jnp.stack([x_rows, grad_rows])
    mirrored = to_mirror(jnp.where(lower, stacked[:, :, half:], stacked[:, :, :half]))

    def spread(rows):
        width = rows.shape[-1]
        rows = jnp.broadcast_to(
            rows.reshape(2, in_flight, 1, CAP, width), (2, in_flight, GROUP, CAP, width)
        ).reshape(2, axis_width, CAP, width)
        rows = lax.all_to_all(rows, "expert", split_axis=1, concat_axis=1, tiled=True)
        return rows.reshape(2, axis_width * CAP, width)

    arrived = spread(stacked)
    d_gate, d_up, hidden = expert_activations(
        arrived[0], arrived[1], w_gate[0], w_up[0], w_down[0]
    )
    activations = jnp.stack([d_gate, d_up, hidden])
    other_activations = to_mirror(activations)
    row_grad = contract(d_gate, w_gate[0], 1, 1) + contract(d_up, w_up[0], 1, 1)
    returned = lax.all_to_all(
        row_grad.reshape(axis_width, CAP, features),
        "expert",
        split_axis=0,
        concat_axis=0,
        tiled=True,
    )
    summed = jnp.sum(returned.reshape(in_flight, GROUP, CAP, features), axis=1).reshape(
        in_flight * CAP, features
    )
    tokens_grad = lax.dot_general(
        select,
        summed,
        (((0,), (0,)), ((), ())),
        precision=lax.Precision.HIGHEST,
        preferred_element_type=jnp.float32,
    )
    tokens_grad = tokens_grad.astype(jnp.bfloat16)
    other = spread(mirrored)
    kept = jnp.where(lower, arrived[:, :, :half], arrived[:, :, half:])
    rows = jnp.concatenate([kept, other], axis=1)
    right = jnp.concatenate([activations, other_activations], axis=1)
    weight_grads = jnp.stack(
        [
            contract(rows[0], right[0], 0, 0),
            contract(rows[0], right[1], 0, 0),
            contract(rows[1], right[2], 0, 0),
        ]
    ).astype(jnp.bfloat16)
    return (tokens_grad, weight_grads[None])


def exchange_kernel(
    own, wg_hbm, wu_hbm, wd_hbm,
    rows_out, acts_out, summed_out,
    wg, wu, wd, rows, half_rows, mirror_rows, acts, other_acts, parts, returned,
    load_sem, row_send, row_recv, half_send, half_recv, mirror_send, mirror_recv,
    acts_send, acts_recv, part_send, part_recv,
):
    group = rows.shape[0]
    features = own.shape[1]
    half = features // 2
    me = lax.axis_index("expert")
    section = lax.axis_index("pipe")
    sections = lax.axis_size("pipe")
    opposite = sections - 1 - section
    kept = pl.multiple_of(half * (section // (sections // 2)), 128)
    sent = pl.multiple_of(half - kept, 128)

    loads = [
        pltpu.make_async_copy(source.at[0], target, load_sem.at[i])
        for i, (source, target) in enumerate(((wg_hbm, wg), (wu_hbm, wu), (wd_hbm, wd)))
    ]
    for load in loads:
        load.start()

    def peer(step):
        return lax.rem(me + step, group)

    def from_peer(step):
        return lax.rem(me + group - step, group)

    def to_peers(source, target, send, recv):
        return [
            pltpu.make_async_remote_copy(
                src_ref=source(peer(step)), dst_ref=target.at[me],
                send_sem=send.at[step], recv_sem=recv.at[step],
                device_id={"expert": peer(step)}, device_id_type=MESH,
            )
            for step in range(1, group)
        ]

    def arrivals(target, send, recv):
        for step in range(1, group):
            source = from_peer(step)
            pltpu.make_async_remote_copy(
                src_ref=target.at[source], dst_ref=target.at[source],
                send_sem=send.at[step], recv_sem=recv.at[step],
                device_id={"expert": source}, device_id_type=MESH,
            ).wait_recv()

    barrier = pltpu.get_barrier_semaphore()
    for step in range(1, group):
        pl.semaphore_signal(
            barrier, inc=1, device_id={"expert": peer(step)}, device_id_type=MESH
        )
    pl.semaphore_signal(barrier, inc=1, device_id={"pipe": opposite}, device_id_type=MESH)
    pl.semaphore_wait(barrier, group)

    half_copy = pltpu.make_async_remote_copy(
        src_ref=own.at[:, pl.ds(sent, half)], dst_ref=half_rows,
        send_sem=half_send, recv_sem=half_recv,
        device_id={"pipe": opposite}, device_id_type=MESH,
    )
    half_copy.start()
    row_copies = to_peers(lambda _: own, rows, row_send, row_recv)
    for copy in row_copies:
        copy.start()
    rows[me] = own[...]
    half_copy.wait_recv()
    mirror_copies = to_peers(lambda _: half_rows, mirror_rows, mirror_send, mirror_recv)
    for copy in mirror_copies:
        copy.start()
    mirror_rows[me] = half_rows[...]
    for load in loads:
        load.wait()
    arrivals(rows, row_send, row_recv)

    both = rows[...].reshape(group * 2 * CAP, features)

    def part_of(product, which):
        split = product.reshape(group, 2 * CAP, product.shape[1])
        return split[:, which * CAP : (which + 1) * CAP].reshape(group * CAP, -1)

    gate = part_of(jnp.dot(both, wg[...], preferred_element_type=jnp.float32), 0)
    up = part_of(jnp.dot(both, wu[...], preferred_element_type=jnp.float32), 0)
    back = part_of(contract(both, wd[...], 1, 1), 1)
    sigmoid_gate = jax.nn.sigmoid(gate)
    activated = gate * sigmoid_gate
    d_gate = (back * up * sigmoid_gate * (1.0 + gate * (1.0 - sigmoid_gate))).astype(jnp.bfloat16)
    d_up = (back * activated).astype(jnp.bfloat16)
    acts[0] = d_gate
    acts[1] = d_up
    acts[2] = (activated * up).astype(jnp.bfloat16)
    acts_copy = pltpu.make_async_remote_copy(
        src_ref=acts, dst_ref=other_acts,
        send_sem=acts_send, recv_sem=acts_recv,
        device_id={"pipe": opposite}, device_id_type=MESH,
    )
    acts_copy.start()

    def row_grad(start):
        columns = pl.ds(start, TILE)
        tile = contract(d_gate, wg[columns, :], 1, 1) + contract(d_up, wu[columns, :], 1, 1)
        return tile.reshape(group, CAP, TILE)

    for start in range(0, half, TILE):
        tile = jnp.concatenate([row_grad(start), row_grad(half + start)], axis=1)
        parts[:, :, start : start + TILE] = tile.astype(jnp.bfloat16)
    part_copies = to_peers(lambda index: parts.at[index], returned, part_send, part_recv)
    for copy in part_copies:
        copy.start()
    returned[me] = parts[me]

    rows_out[0:group] = rows[:, :, pl.ds(kept, half)]
    acts_out[0] = acts[...]
    arrivals(mirror_rows, mirror_send, mirror_recv)
    rows_out[group : 2 * group] = mirror_rows[...]
    acts_copy.wait_recv()
    acts_out[1] = other_acts[...]
    arrivals(returned, part_send, part_recv)
    total = returned[0].astype(jnp.float32)
    for index in range(1, group):
        total = total + returned[index].astype(jnp.float32)
    summed_out[...] = total
    half_copy.wait_send()
    acts_copy.wait_send()
    for copy in row_copies + mirror_copies + part_copies:
        copy.wait_send()


def exchange(own, w_gate, w_up, w_down):
    group = lax.axis_size("expert")
    features = own.shape[1]
    half = features // 2
    hidden = w_gate.shape[2]
    slots = group * CAP
    vmem = pl.BlockSpec(memory_space=pltpu.VMEM)
    anywhere = pl.BlockSpec(memory_space=pl.ANY)
    bf16 = jnp.bfloat16
    dma = pltpu.SemaphoreType.DMA
    return pl.pallas_call(
        exchange_kernel,
        out_shape=(
            jax.ShapeDtypeStruct((2 * group, 2 * CAP, half), bf16),
            jax.ShapeDtypeStruct((2, 3, slots, hidden), bf16),
            jax.ShapeDtypeStruct((2 * CAP, half), jnp.float32),
        ),
        in_specs=[vmem, anywhere, anywhere, anywhere],
        out_specs=(vmem, vmem, vmem),
        scratch_shapes=[
            pltpu.VMEM((features, hidden), bf16),
            pltpu.VMEM((features, hidden), bf16),
            pltpu.VMEM((hidden, features), bf16),
            pltpu.VMEM((group, 2 * CAP, features), bf16),
            pltpu.VMEM((2 * CAP, half), bf16),
            pltpu.VMEM((group, 2 * CAP, half), bf16),
            pltpu.VMEM((3, slots, hidden), bf16),
            pltpu.VMEM((3, slots, hidden), bf16),
            pltpu.VMEM((group, 2 * CAP, half), bf16),
            pltpu.VMEM((group, 2 * CAP, half), bf16),
            dma((3,)),
            dma((group,)),
            dma((group,)),
            dma,
            dma,
            dma((group,)),
            dma((group,)),
            dma,
            dma,
            dma((group,)),
            dma((group,)),
        ],
        compiler_params=pltpu.CompilerParams(
            collective_id=0, has_side_effects=True, vmem_limit_bytes=40 * 1024 * 1024
        ),
    )(own, w_gate, w_up, w_down)


def kernel_body(tokens, out_grad, probs, expert_ids, w_gate, w_up, w_down):
    half = tokens.shape[1] // 2
    select, slot_weight = route_slots(expert_ids, probs, 1)
    picker = select.astype(jnp.bfloat16)
    x_rows = jnp.dot(picker, tokens, preferred_element_type=jnp.float32)
    grad_rows = jnp.dot(picker, out_grad, preferred_element_type=jnp.float32)
    own = jnp.concatenate([x_rows, grad_rows * slot_weight[:, None]]).astype(jnp.bfloat16)
    rows, acts, summed = exchange(own, w_gate, w_up, w_down)
    summed = jnp.concatenate([summed[:CAP], summed[CAP:]], axis=1)
    tokens_grad = lax.dot_general(
        select,
        summed,
        (((0,), (0,)), ((), ())),
        precision=lax.Precision.HIGHEST,
        preferred_element_type=jnp.float32,
    ).astype(jnp.bfloat16)
    x_all = rows[:, :CAP].reshape(-1, half)
    grad_all = rows[:, CAP:].reshape(-1, half)
    right = [acts[:, i].reshape(-1, acts.shape[3]) for i in range(3)]
    weight_grads = jnp.stack(
        [
            contract(x_all, right[0], 0, 0),
            contract(x_all, right[1], 0, 0),
            contract(grad_all, right[2], 0, 0),
        ]
    ).astype(jnp.bfloat16)
    return (tokens_grad, weight_grads[None])


def solution(mesh):
    single = mesh.shape["expert"] == GROUP
    return jax.shard_map(
        kernel_body if single else body,
        mesh=mesh,
        in_specs=(
            P(("pipe", "expert"), None),
            P(("pipe", "expert"), None),
            P(("pipe", "expert"), None),
            P(("pipe", "expert"), None),
            P("pipe", None, "expert"),
            P("pipe", None, "expert"),
            P("pipe", "expert", None),
        ),
        out_specs=(P(("pipe", "expert"), None), P("pipe", None, None, "expert")),
        check_vma=False,
    )
```

```python
import jax
import jax.numpy as jnp
from jax import lax
from jax.experimental import pallas as pl
from jax.experimental.pallas import tpu as pltpu
from jax.sharding import PartitionSpec as P

GROUP = 8
CAP = 8
MESH = pl.DeviceIdType.MESH
TILE = 256


def route_slots(block_ids, block_probs, in_flight):
    experts = jnp.arange(in_flight, dtype=jnp.int32)
    hits = block_ids[:, :, None] == experts[None, None, :]
    member = jnp.any(hits, axis=1).astype(jnp.int32)
    chosen = jnp.sum(
        jnp.where(hits, block_probs.astype(jnp.float32)[:, :, None], jnp.float32(0.0)), axis=1
    )
    position = jnp.cumsum(member, axis=0) - member
    slots = jnp.arange(CAP, dtype=jnp.int32)
    select = (member.T[:, None, :] == 1) & (position.T[:, None, :] == slots[None, :, None])
    select = select.astype(jnp.float32)
    slot_weight = jnp.einsum("ect,te->ec", select, chosen, precision=lax.Precision.HIGHEST)
    return (select.reshape(in_flight * CAP, -1), slot_weight.reshape(in_flight * CAP))


def contract(left, right, left_dim, right_dim):
    return lax.dot_general(
        left, right, (((left_dim,), (right_dim,)), ((), ())), preferred_element_type=jnp.float32
    )


def to_mirror(value):
    count = lax.axis_size("pipe")
    return lax.ppermute(value, "pipe", [(k, count - 1 - k) for k in range(count)])


def expert_activations(x_rows, grad_rows, gate_cols, up_cols, down_rows):
    gate = jnp.dot(x_rows, gate_cols, preferred_element_type=jnp.float32)
    up = jnp.dot(x_rows, up_cols, preferred_element_type=jnp.float32)
    sigmoid_gate = jax.nn.sigmoid(gate)
    activated = gate * sigmoid_gate
    hidden = (activated * up).astype(jnp.bfloat16)
    back = contract(grad_rows, down_rows, 1, 1)
    d_gate = (back * up * sigmoid_gate * (1.0 + gate * (1.0 - sigmoid_gate))).astype(jnp.bfloat16)
    d_up = (back * activated).astype(jnp.bfloat16)
    return d_gate, d_up, hidden


def body(tokens, out_grad, probs, expert_ids, w_gate, w_up, w_down):
    axis_width = lax.axis_size("expert")
    in_flight = axis_width // GROUP
    features = tokens.shape[1]
    half = features // 2
    lower = lax.axis_index("pipe") < lax.axis_size("pipe") // 2
    select, slot_weight = route_slots(expert_ids, probs, in_flight)
    picker = select.astype(jnp.bfloat16)
    x_rows = jnp.dot(picker, tokens, preferred_element_type=jnp.float32).astype(jnp.bfloat16)
    grad_rows = (
        jnp.dot(picker, out_grad, preferred_element_type=jnp.float32) * slot_weight[:, None]
    ).astype(jnp.bfloat16)
    stacked = jnp.stack([x_rows, grad_rows])
    mirrored = to_mirror(jnp.where(lower, stacked[:, :, half:], stacked[:, :, :half]))

    def spread(rows):
        width = rows.shape[-1]
        rows = jnp.broadcast_to(
            rows.reshape(2, in_flight, 1, CAP, width), (2, in_flight, GROUP, CAP, width)
        ).reshape(2, axis_width, CAP, width)
        rows = lax.all_to_all(rows, "expert", split_axis=1, concat_axis=1, tiled=True)
        return rows.reshape(2, axis_width * CAP, width)

    arrived = spread(stacked)
    d_gate, d_up, hidden = expert_activations(
        arrived[0], arrived[1], w_gate[0], w_up[0], w_down[0]
    )
    activations = jnp.stack([d_gate, d_up, hidden])
    other_activations = to_mirror(activations)
    row_grad = contract(d_gate, w_gate[0], 1, 1) + contract(d_up, w_up[0], 1, 1)
    returned = lax.all_to_all(
        row_grad.reshape(axis_width, CAP, features),
        "expert",
        split_axis=0,
        concat_axis=0,
        tiled=True,
    )
    summed = jnp.sum(returned.reshape(in_flight, GROUP, CAP, features), axis=1).reshape(
        in_flight * CAP, features
    )
    tokens_grad = lax.dot_general(
        select,
        summed,
        (((0,), (0,)), ((), ())),
        precision=lax.Precision.HIGHEST,
        preferred_element_type=jnp.float32,
    )
    tokens_grad = tokens_grad.astype(jnp.bfloat16)
    other = spread(mirrored)
    kept = jnp.where(lower, arrived[:, :, :half], arrived[:, :, half:])
    rows = jnp.concatenate([kept, other], axis=1)
    right = jnp.concatenate([activations, other_activations], axis=1)
    weight_grads = jnp.stack(
        [
            contract(rows[0], right[0], 0, 0),
            contract(rows[0], right[1], 0, 0),
            contract(rows[1], right[2], 0, 0),
        ]
    ).astype(jnp.bfloat16)
    return (tokens_grad, weight_grads[None])


def exchange_kernel(
    own, wg_hbm, wu_hbm, wd_hbm,
    rows_out, acts_out, summed_out,
    wg, wu, wd, rows, half_rows, mirror_rows, acts, other_acts, parts, returned,
    load_sem, row_send, row_recv, half_send, half_recv, mirror_send, mirror_recv,
    acts_send, acts_recv, part_send, part_recv,
):
    group = rows.shape[0]
    features = own.shape[1]
    half = features // 2
    me = lax.axis_index("expert")
    section = lax.axis_index("pipe")
    sections = lax.axis_size("pipe")
    opposite = sections - 1 - section
    kept = pl.multiple_of(half * (section // (sections // 2)), 128)
    sent = pl.multiple_of(half - kept, 128)

    loads = [
        pltpu.make_async_copy(source.at[0], target, load_sem.at[i])
        for i, (source, target) in enumerate(((wg_hbm, wg), (wu_hbm, wu), (wd_hbm, wd)))
    ]
    for load in loads:
        load.start()

    def peer(step):
        return lax.rem(me + step, group)

    def from_peer(step):
        return lax.rem(me + group - step, group)

    def to_peers(source, target, send, recv):
        return [
            pltpu.make_async_remote_copy(
                src_ref=source(peer(step)), dst_ref=target.at[me],
                send_sem=send.at[step], recv_sem=recv.at[step],
                device_id={"expert": peer(step)}, device_id_type=MESH,
            )
            for step in range(1, group)
        ]

    def arrivals(target, send, recv):
        for step in range(1, group):
            source = from_peer(step)
            pltpu.make_async_remote_copy(
                src_ref=target.at[source], dst_ref=target.at[source],
                send_sem=send.at[step], recv_sem=recv.at[step],
                device_id={"expert": source}, device_id_type=MESH,
            ).wait_recv()

    chips = group // 2
    sibling = me + 1 - 2 * lax.rem(me, 2)

    def share(source, target, send, recv, index, slot, device):
        return pltpu.make_async_remote_copy(
            src_ref=source, dst_ref=target.at[slot],
            send_sem=send.at[index], recv_sem=recv.at[index],
            device_id={"expert": device}, device_id_type=MESH,
        )

    def spread(source, target, send, recv):
        copies = [
            share(source, target, send, recv, chip, me, peer(2 * chip))
            for chip in range(1, chips)
        ]
        copies.append(share(source, target, send, recv, 0, me, sibling))
        for copy in copies:
            copy.start()
        return copies

    def relay(target, send, recv):
        copies = []
        for chip in range(1, chips):
            slot = from_peer(2 * chip)
            share(target.at[slot], target, send, recv, chip, slot, slot).wait_recv()
            copy = share(target.at[slot], target, send, recv, chips + chip, slot, sibling)
            copy.start()
            copies.append(copy)
        return copies

    def relayed(target, send, recv):
        share(target.at[sibling], target, send, recv, 0, sibling, sibling).wait_recv()
        for chip in range(1, chips):
            slot = lax.rem(sibling + group - 2 * chip, group)
            share(target.at[slot], target, send, recv, chips + chip, slot, sibling).wait_recv()

    barrier = pltpu.get_barrier_semaphore()
    for step in range(1, group):
        pl.semaphore_signal(
            barrier, inc=1, device_id={"expert": peer(step)}, device_id_type=MESH
        )
    pl.semaphore_signal(barrier, inc=1, device_id={"pipe": opposite}, device_id_type=MESH)
    pl.semaphore_wait(barrier, group)

    half_copy = pltpu.make_async_remote_copy(
        src_ref=own.at[:, pl.ds(sent, half)], dst_ref=half_rows,
        send_sem=half_send, recv_sem=half_recv,
        device_id={"pipe": opposite}, device_id_type=MESH,
    )
    half_copy.start()
    row_copies = spread(own, rows, row_send, row_recv)
    rows[me] = own[...]
    half_copy.wait_recv()
    mirror_copies = spread(half_rows, mirror_rows, mirror_send, mirror_recv)
    mirror_rows[me] = half_rows[...]
    row_copies += relay(rows, row_send, row_recv)
    for load in loads:
        load.wait()
    relayed(rows, row_send, row_recv)

    both = rows[...].reshape(group * 2 * CAP, features)

    def part_of(product, which):
        split = product.reshape(group, 2 * CAP, product.shape[1])
        return split[:, which * CAP : (which + 1) * CAP].reshape(group * CAP, -1)

    gate = part_of(jnp.dot(both, wg[...], preferred_element_type=jnp.float32), 0)
    up = part_of(jnp.dot(both, wu[...], preferred_element_type=jnp.float32), 0)
    back = part_of(contract(both, wd[...], 1, 1), 1)
    sigmoid_gate = jax.nn.sigmoid(gate)
    activated = gate * sigmoid_gate
    d_gate = (back * up * sigmoid_gate * (1.0 + gate * (1.0 - sigmoid_gate))).astype(jnp.bfloat16)
    d_up = (back * activated).astype(jnp.bfloat16)
    acts[0] = d_gate
    acts[1] = d_up
    acts[2] = (activated * up).astype(jnp.bfloat16)
    acts_copy = pltpu.make_async_remote_copy(
        src_ref=acts, dst_ref=other_acts,
        send_sem=acts_send, recv_sem=acts_recv,
        device_id={"pipe": opposite}, device_id_type=MESH,
    )
    acts_copy.start()
    mirror_copies += relay(mirror_rows, mirror_send, mirror_recv)

    def row_grad(start):
        columns = pl.ds(start, TILE)
        tile = contract(d_gate, wg[columns, :], 1, 1) + contract(d_up, wu[columns, :], 1, 1)
        return tile.reshape(group, CAP, TILE)

    for start in range(0, half, TILE):
        tile = jnp.concatenate([row_grad(start), row_grad(half + start)], axis=1)
        parts[:, :, start : start + TILE] = tile.astype(jnp.bfloat16)
    part_copies = to_peers(lambda index: parts.at[index], returned, part_send, part_recv)
    for copy in part_copies:
        copy.start()
    returned[me] = parts[me]

    rows_out[0:group] = rows[:, :, pl.ds(kept, half)]
    acts_out[0] = acts[...]
    relayed(mirror_rows, mirror_send, mirror_recv)
    rows_out[group : 2 * group] = mirror_rows[...]
    acts_copy.wait_recv()
    acts_out[1] = other_acts[...]
    arrivals(returned, part_send, part_recv)
    total = returned[0].astype(jnp.float32)
    for index in range(1, group):
        total = total + returned[index].astype(jnp.float32)
    summed_out[...] = total
    half_copy.wait_send()
    acts_copy.wait_send()
    for copy in row_copies + mirror_copies + part_copies:
        copy.wait_send()


def exchange(own, w_gate, w_up, w_down):
    group = lax.axis_size("expert")
    features = own.shape[1]
    half = features // 2
    hidden = w_gate.shape[2]
    slots = group * CAP
    vmem = pl.BlockSpec(memory_space=pltpu.VMEM)
    anywhere = pl.BlockSpec(memory_space=pl.ANY)
    bf16 = jnp.bfloat16
    dma = pltpu.SemaphoreType.DMA
    return pl.pallas_call(
        exchange_kernel,
        out_shape=(
            jax.ShapeDtypeStruct((2 * group, 2 * CAP, half), bf16),
            jax.ShapeDtypeStruct((2, 3, slots, hidden), bf16),
            jax.ShapeDtypeStruct((2 * CAP, half), jnp.float32),
        ),
        in_specs=[vmem, anywhere, anywhere, anywhere],
        out_specs=(vmem, vmem, vmem),
        scratch_shapes=[
            pltpu.VMEM((features, hidden), bf16),
            pltpu.VMEM((features, hidden), bf16),
            pltpu.VMEM((hidden, features), bf16),
            pltpu.VMEM((group, 2 * CAP, features), bf16),
            pltpu.VMEM((2 * CAP, half), bf16),
            pltpu.VMEM((group, 2 * CAP, half), bf16),
            pltpu.VMEM((3, slots, hidden), bf16),
            pltpu.VMEM((3, slots, hidden), bf16),
            pltpu.VMEM((group, 2 * CAP, half), bf16),
            pltpu.VMEM((group, 2 * CAP, half), bf16),
            dma((3,)),
            dma((group,)),
            dma((group,)),
            dma,
            dma,
            dma((group,)),
            dma((group,)),
            dma,
            dma,
            dma((group,)),
            dma((group,)),
        ],
        compiler_params=pltpu.CompilerParams(
            collective_id=0, has_side_effects=True, vmem_limit_bytes=58 * 1024 * 1024
        ),
    )(own, w_gate, w_up, w_down)


def kernel_body(tokens, out_grad, probs, expert_ids, w_gate, w_up, w_down):
    half = tokens.shape[1] // 2
    select, slot_weight = route_slots(expert_ids, probs, 1)
    picker = select.astype(jnp.bfloat16)
    x_rows = jnp.dot(picker, tokens, preferred_element_type=jnp.float32)
    grad_rows = jnp.dot(picker, out_grad, preferred_element_type=jnp.float32)
    own = jnp.concatenate([x_rows, grad_rows * slot_weight[:, None]]).astype(jnp.bfloat16)
    rows, acts, summed = exchange(own, w_gate, w_up, w_down)
    summed = jnp.concatenate([summed[:CAP], summed[CAP:]], axis=1)
    tokens_grad = lax.dot_general(
        select,
        summed,
        (((0,), (0,)), ((), ())),
        precision=lax.Precision.HIGHEST,
        preferred_element_type=jnp.float32,
    ).astype(jnp.bfloat16)
    x_all = rows[:, :CAP].reshape(-1, half)
    grad_all = rows[:, CAP:].reshape(-1, half)
    left = jnp.stack([x_all, x_all, grad_all])
    right = acts.transpose(1, 0, 2, 3).reshape(3, -1, acts.shape[3])
    weight_grads = lax.dot_general(
        left, right, (((1,), (1,)), ((0,), (0,))), preferred_element_type=jnp.float32
    ).astype(jnp.bfloat16)
    return (tokens_grad, weight_grads[None])


def solution(mesh):
    single = mesh.shape["expert"] == GROUP
    return jax.shard_map(
        kernel_body if single else body,
        mesh=mesh,
        in_specs=(
            P(("pipe", "expert"), None),
            P(("pipe", "expert"), None),
            P(("pipe", "expert"), None),
            P(("pipe", "expert"), None),
            P("pipe", None, "expert"),
            P("pipe", None, "expert"),
            P("pipe", "expert", None),
        ),
        out_specs=(P(("pipe", "expert"), None), P("pipe", None, None, "expert")),
        check_vma=False,
    )
```
